32 devices in a mesh: dp: 16 (over z, x, core), seq: 2 (over y).
Axes of the slice: x: 2, y: 2, z: 4, core: 2. Of those that a mesh axis runs over, the one named last changes fastest.
Arguments:
- inputs: float32 [16, 1024, 1088], P('dp', 'seq'), may hold values from -6 to 6
- attend_weight: float32 [1088, 3264], P('dp', 'seq'), may hold values from -0.1875 to 0.1875
- out_weight: float32 [1088, 1088], P('dp', 'seq'), may hold values from -0.75 to 0.75
- up_weight: float32 [1088, 4352], P('dp', 'seq'), may hold values from -0.1875 to 0.1875
- down_weight: float32 [4352, 1088], P('dp', 'seq'), may hold values from -0.09375 to 0.09375
- vectors: float32 [1088, 8], P('dp', 'seq'), may hold values from -1.2 to 1.6
- up_bias: float32 [4352], P(('dp', 'seq')), may hold values from -3 to 3
- cotangent: float32 [16, 1024, 1088], P('dp', 'seq'), may hold values from -6 to 6
Outputs:
- outputs: float32 [16, 1024, 1088], P('dp', 'seq')
- grad_inputs: float32 [16, 1024, 1088], P('dp', 'seq')
- grad_attend: float32 [1088, 3264], P('dp', 'seq')
- grad_out: float32 [1088, 1088], P('dp', 'seq')
- grad_up: float32 [1088, 4352], P('dp', 'seq')
- grad_down: float32 [4352, 1088], P('dp', 'seq')
- grad_vectors: float32 [1088, 8], P('dp', 'seq')
- grad_up_bias: float32 [4352], P(('dp', 'seq'))
The draws below stay inside these ranges and needn't reach their ends.
All inputs are finite; a program needn't handle non-finite values.
Results may differ from the reference program's by a relative error of at most 0.012.
Values may be sent and summed in bfloat16 or wider, within the bound.
A program may use at most 320 MiB of HBM per device.

```python
import math
import jax
import jax.numpy as jnp
from jax import lax

D = 1088
HEADS = 17
FF = 4352
HEAD_DIM = 64
LEN = 1024
SEQS = 16


def draw_vectors(key, part):
    key = jax.random.fold_in(key, 7)
    normal = jax.random.truncated_normal(key, -4.0, 4.0, (D, 8), jnp.float32)
    column = jnp.arange(8)
    gain_cols = (column == 0) | (column == 5)
    return jnp.where(gain_cols[None, :], 1.0 + 0.15 * normal, 0.3 * normal).astype(jnp.float32)


def block_scale(own_key, shape, cuts, low, top_value):
    def one(position, shards_of):
        heights = jax.random.uniform(jax.random.fold_in(jax.random.fold_in(own_key, 6), position), (shards_of,), jnp.float32, low / len(cuts), top_value / len(cuts))
        return jnp.repeat(jnp.exp(heights), shape[position] // shards_of).reshape((-1,) + (1,) * (len(shape) - position - 1))

    level = one(*cuts[0])
    for cut in cuts[1:]:
        level = level * one(*cut)
    return level


def gaussian(rng, dims, scale, most, split=(), held_as=jnp.bfloat16):
    entries = jax.random.normal(rng, dims, jnp.float32) * scale
    if len(split) > 0:
        entries = block_scale(rng, dims, split, -0.22, 0.18) * entries
    return jnp.clip(entries, min=-most, max=most).astype(held_as)


def setup_inputs(seed: int = 0) -> dict:
    key_list = jax.random.split(jax.random.key(seed), 9)
    return {
        "inputs": gaussian(key_list[0], (SEQS, LEN, D), 1.0, 6.0, ((0, 16), (1, 2)), jnp.float32),
        "attend_weight": gaussian(key_list[1], (D, 3 * D), D ** -0.5, 0.1875, ((0, 16), (1, 2)), jnp.float32),
        "out_weight": gaussian(key_list[2], (D, D), (D // 16) ** -0.5, 0.75, ((0, 16), (1, 2)), jnp.float32),
        "up_weight": gaussian(key_list[3], (D, FF), D ** -0.5, 0.1875, ((0, 16), (1, 2)), jnp.float32),
        "down_weight": gaussian(key_list[4], (FF, D), FF ** -0.5, 0.09375, ((0, 16), (1, 2)), jnp.float32),
        "vectors": draw_vectors(jax.random.fold_in(key_list[8], 71), 0),
        "up_bias": gaussian(key_list[6], (FF,), 0.3, 3.0, ((0, 32),), jnp.float32),
        "cotangent": gaussian(key_list[7], (SEQS, LEN, D), 1.0, 6.0, ((0, 16), (1, 2)), jnp.float32),
    }


highest_precision = lax.Precision.HIGHEST

@jax.custom_vjp
def low(v):
    return lax.optimization_barrier(v.astype(jnp.bfloat16)).astype(jnp.float32)

@jax.custom_vjp
def low_back(v):
    return v

def low_keep(v):
    return (low(v), None)

def low_pass(kept, grad):
    return (grad,)

def back_keep(v):
    return (v, None)

def back_low(kept, grad):
    return (low(grad),)
low.defvjp(low_keep, low_pass)
low_back.defvjp(back_keep, back_low)

def layer_norm(values, gain_vec, bias_vec):
    center = values - lax.optimization_barrier(jnp.mean(values, -1, keepdims=True))
    spread = lax.optimization_barrier(jnp.mean(center * center, -1, keepdims=True))
    return center * lax.rsqrt(spread + 1e-05) * gain_vec + bias_vec

def one_block(params, sequence_group):
    attention_weight, output_weight, up_projection_weight, down_projection_weight, column_total, up_projection_bias = params
    group_count = sequence_group.shape[0]
    score_scale = 1.0 / math.sqrt(HEAD_DIM)
    first_normed = low(layer_norm(sequence_group, column_total[:, 0], column_total[:, 1]))
    projected_output = jnp.einsum('tgm,mb->tgb', first_normed, attention_weight, precision=highest_precision)
    query_rows = low(low_back(projected_output[..., :D] + column_total[:, 2]))
    key_rows = low(low_back(projected_output[..., D:2 * D]))
    value_rows = low(low_back(projected_output[..., 2 * D:] + column_total[:, 3]))
    query_rows = query_rows.reshape(group_count, LEN, HEADS, HEAD_DIM)
    key_rows = key_rows.reshape(group_count, LEN, HEADS, HEAD_DIM)
    value_rows = value_rows.reshape(group_count, LEN, HEADS, HEAD_DIM)
    scores = low_back(jnp.einsum('sqhe,skhe->shqk', query_rows, key_rows, precision=highest_precision) * score_scale)
    positions = jnp.arange(LEN)
    causal_mask = positions[None, :] <= positions[:, None]
    scores = jnp.where(causal_mask[None, None], scores, -1e+30)
    attn_probs = jax.nn.softmax(scores, axis=-1)
    mixed_attention = jnp.einsum('shqk,skhe->sqhe', low(attn_probs), value_rows, precision=highest_precision)
    mixed_attention = low(low_back(mixed_attention.reshape(group_count, LEN, D)))
    middle_hidden = sequence_group + low_back(jnp.einsum('tgm,mb->tgb', mixed_attention, output_weight, precision=highest_precision)) + column_total[:, 4]
    second_normed = low(layer_norm(middle_hidden, column_total[:, 5], column_total[:, 6]))
    hidden_before_gelu = low_back(jnp.einsum('cwh,ha->cwa', second_normed, up_projection_weight, precision=highest_precision) + up_projection_bias)
    gelu_output = low(jax.nn.gelu(hidden_before_gelu, approximate=False))
    return middle_hidden + low_back(jnp.einsum('qep,pw->qew', gelu_output, down_projection_weight, precision=highest_precision)) + column_total[:, 7]

def forward(inputs, attend_weight, out_weight, up_weight, down_weight, vectors, up_bias):
    params = (low(attend_weight), low(out_weight), low(up_weight), low(down_weight), low(vectors), low(up_bias))
    per_step = math.gcd(SEQS, max(1, 2048 // LEN))
    grouped = inputs.reshape(SEQS // per_step, per_step, LEN, D)
    stepper = jax.checkpoint(lambda sequence_group: one_block(params, sequence_group))
    return lax.map(stepper, grouped).reshape(SEQS, LEN, D)

def reference(inputs, attend_weight, out_weight, up_weight, down_weight, vectors, up_bias, cotangent):
    outputs, pullback = jax.vjp(forward, inputs.astype(jnp.float32), attend_weight.astype(jnp.float32), out_weight.astype(jnp.float32), up_weight.astype(jnp.float32), down_weight.astype(jnp.float32), vectors.astype(jnp.float32), up_bias.astype(jnp.float32))
    gradients = pullback(cotangent.astype(jnp.float32))
    return (outputs, gradients[0], gradients[1], gradients[2], gradients[3], gradients[4], gradients[5], gradients[6])
```

```python
import functools
import math

import jax
import jax.numpy as jnp
from jax import lax
from jax.experimental import pallas as pl
from jax.experimental.pallas import tpu as pltpu
from jax.sharding import PartitionSpec as P

HEADS = 17
HEAD_DIM = 64
BF = jnp.bfloat16
F32 = jnp.float32


def dot(left, right, dims):
    return lax.dot_general(left, right, (dims, ((), ())), preferred_element_type=F32)


def norm_parts(values):
    center = values - jnp.mean(values, -1, keepdims=True)
    spread = jnp.mean(center * center, -1, keepdims=True)
    inv = lax.rsqrt(spread + 1e-05)
    return center * inv, inv


def norm_grad(normed, inv, gain, upstream):
    scaled = gain * upstream
    first = jnp.mean(scaled, -1, keepdims=True)
    second = jnp.mean(scaled * normed, -1, keepdims=True)
    return (scaled - first - normed * second) * inv


def half_mask(rows, head):
    lane = lax.broadcasted_iota(jnp.int32, (rows, 128), 1)
    return (lane < HEAD_DIM) if head == 0 else (lane >= HEAD_DIM)


def causal(scores, offset):
    rows, cols = scores.shape
    query = lax.broadcasted_iota(jnp.int32, (rows, cols), 0) + offset
    keyp = lax.broadcasted_iota(jnp.int32, (rows, cols), 1)
    return jnp.where(keyp <= query, scores, -1e30)


def attend_kernel(q_ref, k_ref, v_ref, o_ref, l_ref):
    rows = q_ref.shape[1]
    offset = lax.axis_index("seq") * rows
    q, k, v = q_ref[0], k_ref[0], v_ref[0]
    zero = jnp.zeros_like(q)
    outs, logs = [], []
    for head in range(2):
        mask = half_mask(rows, head)
        scores = dot(jnp.where(mask, q, zero), k, ((1,), (1,))) * (1.0 / math.sqrt(HEAD_DIM))
        scores = causal(scores, offset)
        top = jnp.max(scores, -1, keepdims=True)
        raised = jnp.exp(scores - top)
        total = jnp.sum(raised, -1, keepdims=True)
        probs = (raised * (1.0 / total)).astype(BF)
        outs.append(dot(probs, v, ((1,), (0,))))
        logs.append(top + jnp.log(total))
    mask = half_mask(rows, 0)
    o_ref[0] = jnp.where(mask, outs[0], outs[1]).astype(BF)
    l_ref[0] = jnp.where(mask, logs[0], logs[1])


def attend_back_kernel(q_ref, k_ref, v_ref, g_ref, l_ref, dq_ref, dk_ref, dv_ref):
    rows = q_ref.shape[1]
    offset = lax.axis_index("seq") * rows
    q, k, v, g = q_ref[0], k_ref[0], v_ref[0], g_ref[0]
    zero = jnp.zeros_like(q)
    scale = 1.0 / math.sqrt(HEAD_DIM)
    dqs = []
    dk = dv = None
    for head in range(2):
        mask = half_mask(rows, head)
        qm, gm = jnp.where(mask, q, zero), jnp.where(mask, g, zero)
        scores = causal(dot(qm, k, ((1,), (1,))) * scale, offset)
        probs = jnp.exp(scores - l_ref[0, :, head * HEAD_DIM : head * HEAD_DIM + 1])
        grad_probs = dot(gm, v, ((1,), (1,)))
        row_dot = jnp.sum(probs * grad_probs, -1, keepdims=True)
        grad_scores = (probs * (grad_probs - row_dot)).astype(BF)
        low = probs.astype(BF)
        dqs.append(dot(grad_scores, k, ((1,), (0,))) * scale)
        dk_part = dot(grad_scores, qm, ((0,), (0,)))
        dv_part = dot(low, gm, ((0,), (0,)))
        dk = dk_part if dk is None else dk + dk_part
        dv = dv_part if dv is None else dv + dv_part
    dq_ref[0] = jnp.where(half_mask(rows, 0), dqs[0], dqs[1]).astype(BF)
    dk_ref[0] = dk * scale
    dv_ref[0] = dv


def attend(q, k, v):
    seqs, rows, width = q.shape
    length = k.shape[1]
    pairs = width // 128
    small = pl.BlockSpec((1, rows, 128), lambda s, h: (s, 0, h))
    large = pl.BlockSpec((1, length, 128), lambda s, h: (s, 0, h))
    work = seqs * pairs * 2 * rows * length
    return pl.pallas_call(
        attend_kernel,
        grid=(seqs, pairs),
        in_specs=[small, large, large],
        out_specs=[small, small],
        out_shape=[
            jax.ShapeDtypeStruct(q.shape, BF),
            jax.ShapeDtypeStruct(q.shape, F32),
        ],
        compiler_params=pltpu.CompilerParams(vmem_limit_bytes=48 * 2**20),
        cost_estimate=pl.CostEstimate(
            flops=work * 1024, bytes_accessed=8 * q.size + 4 * k.size, transcendentals=work
        ),
    )(q, k, v)


def attend_back(q, k, v, g, logs):
    seqs, rows, width = q.shape
    length = k.shape[1]
    pairs = width // 128
    small = pl.BlockSpec((1, rows, 128), lambda s, h: (s, 0, h))
    large = pl.BlockSpec((1, length, 128), lambda s, h: (s, 0, h))
    work = seqs * pairs * 2 * rows * length
    return pl.pallas_call(
        attend_back_kernel,
        grid=(seqs, pairs),
        in_specs=[small, large, large, small, small],
        out_specs=[small, large, large],
        out_shape=[
            jax.ShapeDtypeStruct(q.shape, BF),
            jax.ShapeDtypeStruct(k.shape, F32),
            jax.ShapeDtypeStruct(k.shape, F32),
        ],
        compiler_params=pltpu.CompilerParams(vmem_limit_bytes=52 * 2**20),
        cost_estimate=pl.CostEstimate(
            flops=work * 2560, bytes_accessed=10 * q.size + 12 * k.size, transcendentals=work
        ),
    )(q, k, v, g, logs)


def exchange(value, axis, size, stride):
    return lax.ppermute(value, axis, [(i, i ^ stride) for i in range(size)])


def scatter_sum(left_blocks, right_pieces, dp, seq):
    tokens, _, rows = left_blocks.shape
    cols = right_pieces.shape[-1]
    me, piece = lax.axis_index("dp"), lax.axis_index("seq")
    pairs = left_blocks.reshape(tokens, dp // 2, 2, rows)
    bit = me % 2

    def pick(which):
        return lax.dynamic_index_in_dim(pairs, which, 2, False).reshape(tokens, dp // 2 * rows)

    def piece_at(which):
        return lax.dynamic_index_in_dim(right_pieces, which, 1, False)

    away, near = pick(1 - bit), pick(bit)
    held = []
    for step in range(seq - 1, -1, -1):
        right = piece_at(piece ^ step)
        sent = dot(away, right, ((0,), (0,))).astype(BF)
        got = exchange(sent, "dp", dp, 1)
        held.append(dot(near, right, ((0,), (0,))) + got.astype(F32))
    held = held[::-1]
    half = seq // 2
    while half >= 1:
        kept = []
        for step in range(half):
            got = exchange(held[step + half].astype(BF), "seq", seq, half)
            kept.append(held[step] + got.astype(F32))
        held, half = kept, half // 2
    total = held[0].reshape(dp // 2, rows, cols)
    stride = 2
    while stride < dp:
        bit = (me // stride) % 2
        split = total.reshape(-1, 2, rows, cols)
        sent = lax.dynamic_index_in_dim(split, 1 - bit, 1, False).astype(BF)
        own = lax.dynamic_index_in_dim(split, bit, 1, False)
        total = own + exchange(sent, "dp", dp, stride).astype(F32)
        stride *= 2
    return total.reshape(rows, cols)


def pad_rows(block):
    extra = -block.shape[0] % 8
    return jnp.pad(block, ((0, extra), (0, 0))) if extra else block


def body(dp, seq, inputs, attend_weight, out_weight, up_weight, down_weight, vectors, up_bias, cotangent):
    seqs, rows, width = inputs.shape
    tokens = seqs * rows
    block = attend_weight.shape[0]
    tall = block + (-block % 8)
    piece = lax.axis_index("seq")
    x = inputs.reshape(tokens, width)
    cot = cotangent.reshape(tokens, width)

    few = jnp.concatenate([vectors.astype(BF).reshape(-1), up_bias.astype(BF)])
    filled = jnp.pad(few, (0, -few.size % 1024)).reshape(-1, 128)
    few = lax.all_gather(filled, ("dp", "seq"), axis=0, tiled=True).reshape(dp * seq, -1)
    vec = few[:, : vectors.size].reshape(dp, seq, block, vectors.shape[1])
    vec = vec.transpose(1, 3, 0, 2).reshape(8, width).astype(F32)
    bias = few[:, vectors.size : vectors.size + up_bias.size].reshape(-1).astype(F32)

    def columns(weight):
        pieces = lax.all_gather(pad_rows(weight.astype(BF)), "seq", axis=0)
        return jnp.concatenate([pieces[i] for i in range(seq)], -1)

    def whole(part):
        return lax.all_gather(part, "dp", axis=0, tiled=True)

    attend_full = whole(columns(attend_weight))
    out_cols, up_cols = columns(out_weight), columns(up_weight)
    joint = whole(jnp.concatenate([out_cols, up_cols], -1))
    out_full, up_full = joint[:, :width], joint[:, width:]
    down_full = whole(columns(down_weight))

    def spread(values):
        blocks = values.reshape(values.shape[0], dp, block)
        return jnp.pad(blocks, ((0, 0), (0, 0), (0, tall - block)))

    def wide(values):
        return spread(values).reshape(values.shape[0], dp * tall)

    def narrow(values):
        return values.reshape(values.shape[0], dp, tall)[:, :, :block].reshape(-1, width)

    normed_one, inv_one = norm_parts(x)
    first = (normed_one * vec[0] + vec[1]).astype(BF)
    every = lax.all_gather(first.reshape(seqs, rows, width), "seq", axis=1, tiled=True)
    length = every.shape[1]
    first_wide = wide(first)
    every_wide = wide(every.reshape(seqs * length, width))
    lanes = -width % 128

    def padded(values, count):
        return jnp.pad(values.reshape(seqs, count, width), ((0, 0), (0, 0), (0, lanes)))

    query = padded((dot(first_wide, attend_full[:, :width], ((1,), (0,))) + vec[2]).astype(BF), rows)
    both = dot(every_wide, attend_full[:, width:], ((1,), (0,)))
    keys = padded(both[:, :width].astype(BF), length)
    vals = padded((both[:, width:] + vec[3]).astype(BF), length)
    mixed, logs = attend(query, keys, vals)
    mixed_low = mixed[..., :width].reshape(tokens, width)
    cot_low = cot.astype(BF)

    out_rows = narrow(out_full.T)
    middle = x + dot(mixed_low, out_full.reshape(dp, tall, width)[:, :block].reshape(width, width), ((1,), (0,))) + vec[4]
    normed_two, inv_two = norm_parts(middle)
    second = (normed_two * vec[5] + vec[6]).astype(BF)
    hidden = dot(wide(second), up_full, ((1,), (0,))) + bias
    cdf = 0.5 * (1.0 + lax.erf(hidden * math.sqrt(0.5)))
    gelu = (hidden * cdf).astype(BF)
    slope = cdf + hidden * (jnp.exp(-0.5 * hidden * hidden) * (1.0 / math.sqrt(2 * math.pi)))
    outputs = middle + dot(gelu, down_full, ((1,), (0,))) + vec[7]

    ff_block = down_weight.shape[0]
    own_down = scatter_sum(
        gelu.reshape(tokens, dp, ff_block), cot_low.reshape(tokens, seq, -1), dp, seq
    )
    hidden_low = (slope * dot(cot_low, down_full, ((1,), (1,)))).astype(BF)
    grad_bias = jnp.sum(hidden_low.astype(F32), 0)
    own_up = scatter_sum(spread(second), hidden_low.reshape(tokens, seq, -1), dp, seq)
    grad_second = narrow(dot(hidden_low, up_full, ((1,), (1,))))
    grad_middle = cot + norm_grad(normed_two, inv_two, vec[5], grad_second)
    middle_low = grad_middle.astype(BF)
    grad_mixed = dot(middle_low, out_rows, ((1,), (0,))).astype(BF)
    own_out = scatter_sum(spread(mixed_low), middle_low.reshape(tokens, seq, -1), dp, seq)

    dq, dk, dv = attend_back(query, keys, vals, padded(grad_mixed, rows), logs)

    def piece_sum(part):
        pieces = part.reshape(seqs, seq, rows, part.shape[-1])
        total = lax.dynamic_index_in_dim(pieces, piece, 1, False)
        for step in range(1, seq):
            sent = lax.dynamic_index_in_dim(pieces, jnp.maximum(piece - step, 0), 1, False)
            got = lax.ppermute(sent[..., :width].astype(BF), "seq", [(i, i - step) for i in range(step, seq)])
            total = total + jnp.pad(got.astype(F32), ((0, 0), (0, 0), (0, lanes)))
        return total[..., :width].astype(BF).reshape(tokens, width)

    query_low = dq[..., :width].reshape(tokens, width)
    key_low, value_low = piece_sum(dk), piece_sum(dv)
    joined = jnp.concatenate([query_low, key_low, value_low], -1)
    own_attend = scatter_sum(spread(first), joined.reshape(tokens, seq, -1), dp, seq)
    grad_first = narrow(dot(joined, attend_full, ((1,), (1,))))
    grad_inputs = grad_middle + norm_grad(normed_one, inv_one, vec[0], grad_first)
    grad_vec = jnp.stack(
        [
            jnp.sum(grad_first * normed_one, 0),
            jnp.sum(grad_first, 0),
            jnp.sum(query_low.astype(F32), 0),
            jnp.sum(value_low.astype(F32), 0),
            jnp.sum(grad_middle, 0),
            jnp.sum(grad_second * normed_two, 0),
            jnp.sum(grad_second, 0),
            jnp.sum(cot, 0),
        ]
    )
    grad_vec = grad_vec.reshape(seq, -1, dp, block).transpose(2, 0, 3, 1).reshape(dp * seq, -1)
    small = jnp.concatenate([grad_vec, grad_bias.reshape(dp * seq, -1)], -1)
    small = lax.psum_scatter(small, ("dp", "seq"), scatter_dimension=0, tiled=True)[0]
    return (
        outputs.reshape(inputs.shape),
        grad_inputs.reshape(inputs.shape),
        own_attend[:block],
        own_out[:block],
        own_up[:block],
        own_down,
        small[: vectors.size].reshape(vectors.shape),
        small[vectors.size :],
    )


def solution(mesh):
    rows, tokens = P("dp", "seq"), P("dp", "seq", None)
    flat = P(("dp", "seq"))
    return jax.shard_map(
        functools.partial(body, mesh.shape["dp"], mesh.shape["seq"]),
        mesh=mesh,
        in_specs=(tokens, rows, rows, rows, rows, rows, flat, tokens),
        out_specs=(tokens, tokens, rows, rows, rows, rows, rows, flat),
        check_vma=False,
    )
```

```python
import functools
import math

import jax
import jax.numpy as jnp
from jax import lax
from jax.experimental import pallas as pl
from jax.experimental.pallas import tpu as pltpu
from jax.sharding import PartitionSpec as P

HEADS = 17
HEAD_DIM = 64
BF = jnp.bfloat16
F32 = jnp.float32


def dot(left, right, dims):
    return lax.dot_general(left, right, (dims, ((), ())), preferred_element_type=F32)


def norm_parts(values):
    center = values - jnp.mean(values, -1, keepdims=True)
    spread = jnp.mean(center * center, -1, keepdims=True)
    inv = lax.rsqrt(spread + 1e-05)
    return center * inv, inv


def norm_grad(normed, inv, gain, upstream):
    scaled = gain * upstream
    first = jnp.mean(scaled, -1, keepdims=True)
    second = jnp.mean(scaled * normed, -1, keepdims=True)
    return (scaled - first - normed * second) * inv


def half_mask(rows, head):
    lane = lax.broadcasted_iota(jnp.int32, (rows, 128), 1)
    return (lane < HEAD_DIM) if head == 0 else (lane >= HEAD_DIM)


def causal(scores, offset):
    rows, cols = scores.shape
    query = lax.broadcasted_iota(jnp.int32, (rows, cols), 0) + offset
    keyp = lax.broadcasted_iota(jnp.int32, (rows, cols), 1)
    return jnp.where(keyp <= query, scores, -1e30)


def attend_kernel(q_ref, k_ref, v_ref, o_ref, l_ref):
    rows = q_ref.shape[1]
    offset = lax.axis_index("seq") * rows
    q, k, v = q_ref[0], k_ref[0], v_ref[0]
    zero = jnp.zeros_like(q)
    outs, logs = [], []
    for head in range(2):
        mask = half_mask(rows, head)
        scores = dot(jnp.where(mask, q, zero), k, ((1,), (1,))) * (1.0 / math.sqrt(HEAD_DIM))
        scores = causal(scores, offset)
        top = jnp.max(scores, -1, keepdims=True)
        raised = jnp.exp(scores - top)
        total = jnp.sum(raised, -1, keepdims=True)
        probs = (raised * (1.0 / total)).astype(BF)
        outs.append(dot(probs, v, ((1,), (0,))))
        logs.append(top + jnp.log(total))
    mask = half_mask(rows, 0)
    o_ref[0] = jnp.where(mask, outs[0], outs[1]).astype(BF)
    l_ref[0] = jnp.where(mask, logs[0], logs[1])


def attend_back_kernel(q_ref, k_ref, v_ref, g_ref, l_ref, dq_ref, dk_ref, dv_ref):
    rows = q_ref.shape[1]
    offset = lax.axis_index("seq") * rows
    q, k, v, g = q_ref[0], k_ref[0], v_ref[0], g_ref[0]
    zero = jnp.zeros_like(q)
    scale = 1.0 / math.sqrt(HEAD_DIM)
    dqs = []
    dk = dv = None
    for head in range(2):
        mask = half_mask(rows, head)
        qm, gm = jnp.where(mask, q, zero), jnp.where(mask, g, zero)
        scores = causal(dot(qm, k, ((1,), (1,))) * scale, offset)
        probs = jnp.exp(scores - l_ref[0, :, head * HEAD_DIM : head * HEAD_DIM + 1])
        grad_probs = dot(gm, v, ((1,), (1,)))
        row_dot = jnp.sum(probs * grad_probs, -1, keepdims=True)
        grad_scores = (probs * (grad_probs - row_dot)).astype(BF)
        low = probs.astype(BF)
        dqs.append(dot(grad_scores, k, ((1,), (0,))) * scale)
        dk_part = dot(grad_scores, qm, ((0,), (0,)))
        dv_part = dot(low, gm, ((0,), (0,)))
        dk = dk_part if dk is None else dk + dk_part
        dv = dv_part if dv is None else dv + dv_part
    dq_ref[0] = jnp.where(half_mask(rows, 0), dqs[0], dqs[1]).astype(BF)
    dk_ref[0] = dk * scale
    dv_ref[0] = dv


def attend(q, k, v):
    seqs, rows, width = q.shape
    length = k.shape[1]
    pairs = width // 128
    small = pl.BlockSpec((1, rows, 128), lambda s, h: (s, 0, h))
    large = pl.BlockSpec((1, length, 128), lambda s, h: (s, 0, h))
    work = seqs * pairs * 2 * rows * length
    return pl.pallas_call(
        attend_kernel,
        grid=(seqs, pairs),
        in_specs=[small, large, large],
        out_specs=[small, small],
        out_shape=[
            jax.ShapeDtypeStruct(q.shape, BF),
            jax.ShapeDtypeStruct(q.shape, F32),
        ],
        compiler_params=pltpu.CompilerParams(vmem_limit_bytes=48 * 2**20),
        cost_estimate=pl.CostEstimate(
            flops=work * 1024, bytes_accessed=8 * q.size + 4 * k.size, transcendentals=work
        ),
    )(q, k, v)


def attend_back(q, k, v, g, logs):
    seqs, rows, width = q.shape
    length = k.shape[1]
    pairs = width // 128
    small = pl.BlockSpec((1, rows, 128), lambda s, h: (s, 0, h))
    large = pl.BlockSpec((1, length, 128), lambda s, h: (s, 0, h))
    work = seqs * pairs * 2 * rows * length
    return pl.pallas_call(
        attend_back_kernel,
        grid=(seqs, pairs),
        in_specs=[small, large, large, small, small],
        out_specs=[small, large, large],
        out_shape=[
            jax.ShapeDtypeStruct(q.shape, BF),
            jax.ShapeDtypeStruct(k.shape, F32),
            jax.ShapeDtypeStruct(k.shape, F32),
        ],
        compiler_params=pltpu.CompilerParams(vmem_limit_bytes=52 * 2**20),
        cost_estimate=pl.CostEstimate(
            flops=work * 2560, bytes_accessed=10 * q.size + 12 * k.size, transcendentals=work
        ),
    )(q, k, v, g, logs)


def exchange(value, axis, size, stride):
    return lax.ppermute(value, axis, [(i, i ^ stride) for i in range(size)])


def scatter_sum(left_blocks, right_pieces, dp, seq):
    tokens, _, rows = left_blocks.shape
    cols = right_pieces.shape[-1]
    me, piece = lax.axis_index("dp"), lax.axis_index("seq")
    pairs = left_blocks.reshape(tokens, dp // 2, 2, rows)
    bit = me % 2

    def pick(which):
        return lax.dynamic_index_in_dim(pairs, which, 2, False).reshape(tokens, dp // 2 * rows)

    def piece_at(which):
        return lax.dynamic_index_in_dim(right_pieces, which, 1, False)

    away, near = pick(1 - bit), pick(bit)
    held = []
    for step in range(seq - 1, -1, -1):
        right = piece_at(piece ^ step)
        sent = dot(away, right, ((0,), (0,))).astype(BF)
        got = exchange(sent, "dp", dp, 1)
        held.append(dot(near, right, ((0,), (0,))) + got.astype(F32))
    held = held[::-1]
    half = seq // 2
    while half >= 1:
        kept = []
        for step in range(half):
            got = exchange(held[step + half].astype(BF), "seq", seq, half)
            kept.append(held[step] + got.astype(F32))
        held, half = kept, half // 2
    total = held[0].reshape(dp // 2, rows, cols)
    stride = 2
    while stride < dp:
        bit = (me // stride) % 2
        split = total.reshape(-1, 2, rows, cols)
        sent = lax.dynamic_index_in_dim(split, 1 - bit, 1, False).astype(BF)
        own = lax.dynamic_index_in_dim(split, bit, 1, False)
        total = own + exchange(sent, "dp", dp, stride).astype(F32)
        stride *= 2
    return total.reshape(rows, cols)


def pad_rows(block):
    extra = -block.shape[0] % 8
    return jnp.pad(block, ((0, extra), (0, 0))) if extra else block


def body(dp, seq, inputs, attend_weight, out_weight, up_weight, down_weight, vectors, up_bias, cotangent):
    seqs, rows, width = inputs.shape
    tokens = seqs * rows
    block = attend_weight.shape[0]
    tall = block + (-block % 8)
    piece = lax.axis_index("seq")
    x = inputs.reshape(tokens, width)
    cot = cotangent.reshape(tokens, width)

    def columns(weight):
        pieces = lax.all_gather(pad_rows(weight.astype(BF)), "seq", axis=0)
        return jnp.concatenate([pieces[i] for i in range(seq)], -1)

    attend_cols, vectors, up_bias = lax.optimization_barrier(
        (columns(attend_weight), vectors, up_bias)
    )
    few = jnp.concatenate([vectors.astype(BF).reshape(-1), up_bias.astype(BF)])
    filled = jnp.pad(few, (0, -few.size % 1024)).reshape(-1, 128)
    few = lax.all_gather(filled, ("dp", "seq"), axis=0, tiled=True).reshape(dp * seq, -1)
    vec = few[:, : vectors.size].reshape(dp, seq, block, vectors.shape[1])
    vec = vec.transpose(1, 3, 0, 2).reshape(8, width).astype(F32)
    bias = few[:, vectors.size : vectors.size + up_bias.size].reshape(-1).astype(F32)

    def whole(part):
        return lax.all_gather(part, "dp", axis=0, tiled=True)

    attend_full = whole(attend_cols)
    out_cols, up_cols = columns(out_weight), columns(up_weight)
    joint = whole(jnp.concatenate([out_cols, up_cols], -1))
    out_full, up_full = joint[:, :width], joint[:, width:]
    down_full = whole(columns(down_weight))

    def spread(values):
        blocks = values.reshape(values.shape[0], dp, block)
        return jnp.pad(blocks, ((0, 0), (0, 0), (0, tall - block)))

    def wide(values):
        return spread(values).reshape(values.shape[0], dp * tall)

    def narrow(values):
        return values.reshape(values.shape[0], dp, tall)[:, :, :block].reshape(-1, width)

    normed_one, inv_one = norm_parts(x)
    first = (normed_one * vec[0] + vec[1]).astype(BF)
    every = lax.all_gather(first.reshape(seqs, rows, width), "seq", axis=1, tiled=True)
    length = every.shape[1]
    first_wide = wide(first)
    every_wide = wide(every.reshape(seqs * length, width))
    lanes = -width % 128

    def padded(values, count):
        return jnp.pad(values.reshape(seqs, count, width), ((0, 0), (0, 0), (0, lanes)))

    query = padded((dot(first_wide, attend_full[:, :width], ((1,), (0,))) + vec[2]).astype(BF), rows)
    both = dot(every_wide, attend_full[:, width:], ((1,), (0,)))
    keys = padded(both[:, :width].astype(BF), length)
    vals = padded((both[:, width:] + vec[3]).astype(BF), length)
    mixed, logs = attend(query, keys, vals)
    mixed_low = mixed[..., :width].reshape(tokens, width)
    cot_low = cot.astype(BF)

    out_rows = narrow(out_full.T)
    middle = x + dot(mixed_low, out_full.reshape(dp, tall, width)[:, :block].reshape(width, width), ((1,), (0,))) + vec[4]
    normed_two, inv_two = norm_parts(middle)
    second = (normed_two * vec[5] + vec[6]).astype(BF)
    hidden = dot(wide(second), up_full, ((1,), (0,))) + bias
    cdf = 0.5 * (1.0 + lax.erf(hidden * math.sqrt(0.5)))
    gelu = (hidden * cdf).astype(BF)
    slope = cdf + hidden * (jnp.exp(-0.5 * hidden * hidden) * (1.0 / math.sqrt(2 * math.pi)))
    outputs = middle + dot(gelu, down_full, ((1,), (0,))) + vec[7]

    ff_block = down_weight.shape[0]
    own_down = scatter_sum(
        gelu.reshape(tokens, dp, ff_block), cot_low.reshape(tokens, seq, -1), dp, seq
    )
    hidden_low = (slope * dot(cot_low, down_full, ((1,), (1,)))).astype(BF)
    grad_bias = jnp.sum(hidden_low.astype(F32), 0)
    own_up = scatter_sum(spread(second), hidden_low.reshape(tokens, seq, -1), dp, seq)
    grad_second = narrow(dot(hidden_low, up_full, ((1,), (1,))))
    grad_middle = cot + norm_grad(normed_two, inv_two, vec[5], grad_second)
    middle_low = grad_middle.astype(BF)
    grad_mixed = dot(middle_low, out_rows, ((1,), (0,))).astype(BF)
    own_out = scatter_sum(spread(mixed_low), middle_low.reshape(tokens, seq, -1), dp, seq)

    dq, dk, dv = attend_back(query, keys, vals, padded(grad_mixed, rows), logs)

    def piece_sum(part):
        pieces = part.reshape(seqs, seq, rows, part.shape[-1])
        total = lax.dynamic_index_in_dim(pieces, piece, 1, False)
        for step in range(1, seq):
            sent = lax.dynamic_index_in_dim(pieces, jnp.maximum(piece - step, 0), 1, False)
            got = lax.ppermute(sent[..., :width].astype(BF), "seq", [(i, i - step) for i in range(step, seq)])
            total = total + jnp.pad(got.astype(F32), ((0, 0), (0, 0), (0, lanes)))
        return total[..., :width].astype(BF).reshape(tokens, width)

    query_low = dq[..., :width].reshape(tokens, width)
    key_low, value_low = piece_sum(dk), piece_sum(dv)
    joined = jnp.concatenate([query_low, key_low, value_low], -1)
    own_attend = scatter_sum(spread(first), joined.reshape(tokens, seq, -1), dp, seq)
    grad_first = narrow(dot(joined, attend_full, ((1,), (1,))))
    grad_inputs = grad_middle + norm_grad(normed_one, inv_one, vec[0], grad_first)
    grad_vec = jnp.stack(
        [
            jnp.sum(grad_first * normed_one, 0),
            jnp.sum(grad_first, 0),
            jnp.sum(query_low.astype(F32), 0),
            jnp.sum(value_low.astype(F32), 0),
            jnp.sum(grad_middle, 0),
            jnp.sum(grad_second * normed_two, 0),
            jnp.sum(grad_second, 0),
            jnp.sum(cot, 0),
        ]
    )
    grad_vec = grad_vec.reshape(seq, -1, dp, block).transpose(2, 0, 3, 1).reshape(dp * seq, -1)
    small = jnp.concatenate([grad_vec, grad_bias.reshape(dp * seq, -1)], -1)
    small = lax.psum_scatter(small, ("dp", "seq"), scatter_dimension=0, tiled=True)[0]
    return (
        outputs.reshape(inputs.shape),
        grad_inputs.reshape(inputs.shape),
        own_attend[:block],
        own_out[:block],
        own_up[:block],
        own_down,
        small[: vectors.size].reshape(vectors.shape),
        small[vectors.size :],
    )


def solution(mesh):
    rows, tokens = P("dp", "seq"), P("dp", "seq", None)
    flat = P(("dp", "seq"))
    return jax.shard_map(
        functools.partial(body, mesh.shape["dp"], mesh.shape["seq"]),
        mesh=mesh,
        in_specs=(tokens, rows, rows, rows, rows, rows, flat, tokens),
        out_specs=(tokens, tokens, rows, rows, rows, rows, rows, flat),
        check_vma=False,
    )
```
